512 devices in a mesh: dp: 32 (over y, z_lo, core), inv: 16 (over z_hi, x).
Axes of the slice: x: 4, y: 4, z: 16 (z_hi: 4, z_lo: 4; z = z_hi * 4 + z_lo), core: 2. Of those that a mesh axis runs over, the one named last changes fastest.
Arguments:
- acts: bfloat16 [4096, 6144], P('dp', 'inv'), may hold values from -6 to 6
- grads_out: bfloat16 [4096, 24576], P('inv', 'dp'), may hold values from -0.119628906 to 0.119628906
- scale_exp: int32 [4096], replicated, may hold values from 0 to 3
- shard_tokens: int32 [32], replicated, may hold values from 1 to 128, 3072 in all
Outputs:
- precond: bfloat16 [6144, 24576], P('inv', 'dp')
The draws below stay inside these ranges and needn't reach their ends.
Inputs may be any that keep to these rules, and one draw needn't show every extreme that they name: `shard_tokens`: largest entry is exactly 128; entries sum to 3072.
All inputs are finite; a program needn't handle non-finite values.
Results may differ from the reference program's by a relative error of at most 0.0015.
Values may be sent and summed in bfloat16 or wider, within the bound.
No kernel may reach another device: no remote copies, remote signals or barrier semaphores. Data moves between devices by JAX's collectives and lax.ppermute only.
A program may use at most 64 MiB of HBM per device.

```python
import math
import jax
import jax.numpy as jnp
import numpy as np
from jax import lax

D = 6144
FF = 24576
BLK = 128
ITERS = 8
TOK_DEV = 128
TOKENS = 4096
VALID = 3072
N_DP = 32


def set_ends(result, stream_key, least, high):
    longest = result.shape.index(max(result.shape))
    spots = []
    for shift in (0, 1):
        where = [jax.random.randint(jax.random.fold_in(stream_key, axis), (), 0, length) for axis, length in enumerate(result.shape)]
        where[longest] = (where[longest] + shift) % result.shape[longest]
        spots.append(tuple(where))
    return result.at[spots[0]].set(least).at[spots[1]].set(high)


def block_levels(rng, shape, split, low, largest):
    def one(axis_at, shards_of):
        steps = jax.random.uniform(jax.random.fold_in(jax.random.fold_in(rng, 6), axis_at), (shards_of,), jnp.float32, low / len(split), largest / len(split))
        return jnp.repeat(jnp.exp(steps), shape[axis_at] // shards_of).reshape((-1,) + (1,) * (len(shape) - axis_at - 1))

    factor_of = one(*split[0])
    for cut in split[1:]:
        factor_of = factor_of * one(*cut)
    return factor_of


def profile(count, total, most, skew):
    loads = [(1 << 20) // math.isqrt(rank ** skew) + 1 for rank in range(2, count + 1)]
    surplus, holding = total - most - (count - 1), [1] * (count - 1)
    while surplus > 0:
        free = [i for i in range(count - 1) if holding[i] < most]
        whole, remaining = sum([loads[i] for i in free]), surplus
        for i in free:
            extra = min(most - holding[i], max(1, remaining * loads[i] // whole), surplus)
            holding[i] = holding[i] + extra
            surplus = surplus - extra
    return np.array([most] + holding)


def uneven(stream_key, amount, total, reach, slope):
    if amount == 2:
        one = jax.random.randint(stream_key, (), max(1, total - reach), min(reach, total - 1) + 1)
        return jnp.stack([one, total - one])
    tallies = jnp.asarray(profile(amount, total, reach, slope), jnp.int32)
    twos = (amount - 1) // 2
    giver, receiver = tallies[1:1 + 2 * twos:2], tallies[2:2 + 2 * twos:2]
    slack = jnp.minimum(giver - 1, reach - receiver)
    passed = jax.random.randint(jax.random.fold_in(stream_key, 1), (twos,), 0, 1 << 20) % (slack + 1)
    tallies = tallies.at[1:1 + 2 * twos:2].set(giver - passed).at[2:2 + 2 * twos:2].set(receiver + passed)
    return tallies[jax.random.permutation(jax.random.fold_in(stream_key, 2), amount)]


def scatter_about(rng, dims, deviation, most, cuts=(), held_as=jnp.bfloat16):
    array = deviation * jax.random.normal(rng, dims, jnp.float32)
    if cuts:
        array = array * block_levels(rng, dims, cuts, -0.22, 0.18)
    return jnp.clip(array, -most, most).astype(held_as)


def setup_inputs(seed: int = 0) -> dict:
    arg_keys = jax.random.split(jax.random.key(seed), 5)
    acts = scatter_about(arg_keys[0], (TOKENS, D), 1.0, 6.0, ((0, 32), (1, 16)))
    grads_out = scatter_about(arg_keys[1], (TOKENS, FF), 0.02, 0.119628906, ((0, 16), (1, 32)))
    scale_exp = set_ends(jax.random.randint(arg_keys[2], (TOKENS,), 0, 4), jax.random.fold_in(arg_keys[2], 1), 0, 3).astype(jnp.int32)
    shard_tokens = uneven(arg_keys[3], N_DP, VALID, TOK_DEV, 2).astype(jnp.int32)
    return {"acts": acts, "grads_out": grads_out, "scale_exp": scale_exp, "shard_tokens": shard_tokens}


damping = 1e-3


def block_cov(rows, order):
    shaped = rows.astype(jnp.float32).reshape(rows.shape[0], rows.shape[1] // order, order)
    return jnp.einsum('tbi,tbj->bij', shaped, shaped, precision=lax.Precision.HIGHEST)


def damped(cov):
    order = cov.shape[-1]
    eye = jnp.eye(order, dtype=jnp.float32)
    trace = jnp.trace(cov, axis1=1, axis2=2)
    return cov + damping * (trace / order)[:, None, None] * eye


def newton(matrix):
    order = matrix.shape[-1]
    eye = jnp.eye(order, dtype=jnp.float32)
    trace = jnp.trace(matrix, axis1=1, axis2=2)
    approx = eye[None] / trace[:, None, None]
    for step in range(ITERS):
        inner = jnp.einsum('bij,bjk->bik', matrix, approx, precision=lax.Precision.HIGHEST)
        approx = jnp.einsum('bij,bjk->bik', approx, 2.0 * eye - inner, precision=lax.Precision.HIGHEST)
    return approx


def reference(acts, grads_out, scale_exp, shard_tokens):
    tokens = acts.shape[0]
    ids = jnp.arange(tokens, dtype=jnp.int32)
    limit = jnp.repeat(shard_tokens, TOK_DEV)
    live = ids % TOK_DEV < limit
    row_weight = jnp.where(live, jnp.exp2(-scale_exp.astype(jnp.float32)), 0.0)
    masked = acts * live.astype(jnp.bfloat16)[:, None]
    scaled = grads_out * row_weight.astype(jnp.bfloat16)[:, None]
    count = jnp.sum(shard_tokens).astype(jnp.float32)
    grad = jnp.dot(masked.T, scaled, preferred_element_type=jnp.float32) / count
    a_inv = newton(damped(block_cov(masked, BLK) / count))
    g_inv = newton(damped(block_cov(scaled, BLK) / count))
    shaped = grad.reshape(D // BLK, BLK, FF // BLK, BLK)
    left = jnp.einsum('bij,bjck->bick', a_inv, shaped, precision=lax.Precision.HIGHEST)
    both = jnp.einsum('bick,ckl->bicl', left, g_inv, precision=lax.Precision.HIGHEST)
    return both.reshape(D, FF).astype(jnp.bfloat16)
```

```python
import functools

import jax
import jax.numpy as jnp
from jax import lax
from jax.experimental import pallas as pl
from jax.experimental.pallas import tpu as pltpu
from jax.sharding import PartitionSpec as P

BLK = 128
TOK_DEV = 128
DAMPING = 0.001
VMEM_LIMIT = 40 * 1024 * 1024


def shift_x(step):
    return [(i, i // 4 * 4 + (i + step) % 4) for i in range(16)]


def shift_z(step):
    return [(i, (i // 4 + step) % 4 * 4 + i % 4) for i in range(16)]


def flip_dp(mask):
    return [(j, j ^ mask) for j in range(32)]


def hop(value, pairs):
    return lax.ppermute(value, "inv", pairs)


def swap(value, mask):
    return lax.ppermute(value, "dp", flip_dp(mask))


def both_ways(value, shift):
    return hop(value, shift(1)), hop(value, shift(-1))


def far_halves(lower, upper, shift):
    half = lower.shape[0] // 2
    return hop(lower[:half], shift(1)), hop(upper[half:], shift(-1))


def eye(order):
    rows = lax.broadcasted_iota(jnp.int32, (order, order), 0)
    cols = lax.broadcasted_iota(jnp.int32, (order, order), 1)
    return rows == cols


def dot32(a, b):
    return jnp.dot(
        a, b, precision=lax.Precision.HIGHEST, preferred_element_type=jnp.float32
    )


def pair_diag(a, b):
    zero = jnp.zeros_like(a)
    return jnp.concatenate(
        [jnp.concatenate([a, zero], 1), jnp.concatenate([zero, b], 1)], 0
    )


def newton(covs):
    unit = eye(BLK)
    ident = unit.astype(jnp.float32)
    errors, approxes = [], []
    for cov in covs:
        trace = jnp.sum(jnp.where(unit, cov, 0.0))
        damped = cov + (DAMPING * (trace / BLK)) * ident
        total = jnp.sum(jnp.where(unit, damped, 0.0))
        error = ident - damped / total
        errors.append(error)
        approxes.append((ident + error) / total)
    if len(covs) % 2:
        errors.append(errors[-1])
        approxes.append(approxes[-1])
    pairs = len(errors) // 2
    err = [jnp.concatenate(errors[2 * p : 2 * p + 2], 1) for p in range(pairs)]
    app = [jnp.concatenate(approxes[2 * p : 2 * p + 2], 1) for p in range(pairs)]

    def spread(wide):
        return pair_diag(wide[:, :BLK], wide[:, BLK:])

    err = [dot32(e, spread(e)) for e in err]
    for step in range(6):
        both = [
            dot32(jnp.concatenate([x, e], 0), spread(e))
            for x, e in zip(app, err, strict=True)
        ]
        app = [x + b[:BLK] for x, b in zip(app, both, strict=True)]
        err = [b[BLK:] for b in both]
    app = [x + dot32(x, spread(e)) for x, e in zip(app, err, strict=True)]
    return [
        app[n // 2][:, n % 2 * BLK : (n % 2 + 1) * BLK] for n in range(len(covs))
    ]


def acts_kernel(where_ref, count_ref, *refs):
    parts, (acts_ref, inv_ref) = refs[:4], refs[4:]
    mine = where_ref[0]
    blocks = acts_ref.shape[2] // BLK
    covs = [jnp.zeros((BLK, BLK), jnp.float32) for _ in range(blocks)]
    for n, part in enumerate(parts):
        for k in range(8):
            zl = (k & 1) ^ (k & 2)
            y = (k >> 2 & 1) ^ (3 if n % 2 else 0)
            mask = y * 8 + zl * 2 + n // 2
            acts_ref[mine ^ mask] = part[k]
        rows = part[...].reshape(8 * TOK_DEV, blocks * BLK)
        flipped = rows.T
        for b in range(blocks):
            cols = slice(b * BLK, (b + 1) * BLK)
            covs[b] += jnp.dot(
                flipped[cols], rows[:, cols], preferred_element_type=jnp.float32
            )
    count = count_ref[0]
    for b, inverse in enumerate(newton([c / count for c in covs])):
        inv_ref[b] = inverse


def add_rows(where_ref, acts_ref, piece, dz, dx, half, sums, first):
    zh, x = where_ref[1], where_ref[2]
    token = ((zh + dz) & 3) * 8 + ((x + dx) & 3) * 2
    if half is None:
        rows = acts_ref[pl.ds(token, 2)].reshape(2 * TOK_DEV, acts_ref.shape[2])
    else:
        rows = acts_ref[token + half]
    wide = rows.shape[1]
    flipped = piece.T
    main = jnp.dot(flipped, rows, preferred_element_type=jnp.float32)
    cov = [
        jnp.dot(
            flipped[f * BLK : (f + 1) * BLK],
            piece[:, f * BLK : (f + 1) * BLK],
            preferred_element_type=jnp.float32,
        )
        for f in range(piece.shape[1] // BLK)
    ]
    cov = jnp.concatenate(cov, 0)
    if first:
        sums[:, :wide] = main
        sums[:, wide:] = cov
    else:
        sums[:, :wide] += main
        sums[:, wide:] += cov


def add_group(where_ref, acts_ref, group, kind, sums, first):
    own, low, high, far_low, far_high = group
    step = 2 * TOK_DEV
    for ref, dx in ((own, 0), (low, -1), (high, 1)):
        if kind == 1:
            for n, dz in ((0, -1), (1, 1)):
                piece = ref[n * step : (n + 1) * step, :]
                add_rows(where_ref, acts_ref, piece, dz, dx, None, sums, first)
                first = False
        else:
            add_rows(where_ref, acts_ref, ref[...], kind, dx, None, sums, first)
            first = False
    for ref, n in ((far_low, 0), (far_high, 1)):
        if kind == 1:
            dz = (-1, 1)[n]
            add_rows(where_ref, acts_ref, ref[...], dz, 2, None, sums, False)
        else:
            add_rows(where_ref, acts_ref, ref[...], kind, 2, n, sums, False)


def first_kernel(kind, where_ref, acts_ref, *refs):
    add_group(where_ref, acts_ref, refs[:5], kind, refs[5], True)


def more_kernel(kind, where_ref, acts_ref, *refs):
    sums = refs[6]
    sums[...] = refs[5][...]
    add_group(where_ref, acts_ref, refs[:5], kind, sums, False)


def last_kernel(kind, where_ref, count_ref, acts_ref, inv_ref, *refs):
    out_ref, sums = refs[6], refs[7]
    sums[...] = refs[5][...]
    add_group(where_ref, acts_ref, refs[:5], kind, sums, False)
    wide = acts_ref.shape[2]
    count = count_ref[0]
    outs = sums.shape[0]
    blocks = outs // BLK
    inverse = newton(
        [sums[f * BLK : (f + 1) * BLK, wide:] / count for f in range(blocks)]
    )
    lefts = []
    for b in range(wide // BLK):
        grad = sums[:, b * BLK : (b + 1) * BLK] / count
        lefts.append(dot32(grad, inv_ref[b].T))
    for f in range(0, blocks, 2):
        right = pair_diag(inverse[f], inverse[f + 1])
        for b in range(wide // BLK):
            left = jnp.concatenate(
                [lefts[b][(f + n) * BLK : (f + n + 1) * BLK].T for n in range(2)], 1
            )
            out_ref[b * BLK : (b + 1) * BLK, f * BLK : (f + 2) * BLK] = dot32(
                left, right
            ).astype(jnp.bfloat16)


def call(kernel, smem, vmem, shapes, scratch=()):
    return pl.pallas_call(
        kernel,
        out_shape=shapes,
        in_specs=[pl.BlockSpec(memory_space=pltpu.SMEM)] * len(smem)
        + [pl.BlockSpec(memory_space=pltpu.VMEM)] * len(vmem),
        out_specs=jax.tree.map(
            lambda _: pl.BlockSpec(memory_space=pltpu.VMEM), shapes
        ),
        scratch_shapes=list(scratch),
        compiler_params=pltpu.CompilerParams(vmem_limit_bytes=VMEM_LIMIT),
    )(*smem, *vmem)


def local(acts, grads_out, scale_exp, shard_tokens):
    dp_index = lax.axis_index("dp")
    inv_index = lax.axis_index("inv")
    rows = grads_out.shape[0]
    wide = acts.shape[1]
    outs = grads_out.shape[1]
    where = jnp.stack([dp_index, inv_index // 4, inv_index % 4]).astype(jnp.int32)
    count = jnp.sum(shard_tokens).astype(jnp.float32)[None]

    exps = lax.dynamic_slice_in_dim(scale_exp, inv_index * rows, rows)
    limit = lax.dynamic_slice_in_dim(shard_tokens, inv_index * 2, 2)
    live = jnp.arange(rows, dtype=jnp.int32) % TOK_DEV < jnp.repeat(limit, TOK_DEV)
    weight = jnp.where(live, jnp.exp2(-exps.astype(jnp.float32)), 0.0)
    scaled = grads_out * weight.astype(jnp.bfloat16)[:, None]
    mine = lax.dynamic_slice_in_dim(shard_tokens, dp_index, 1)
    masked = acts * (jnp.arange(TOK_DEV, dtype=jnp.int32) < mine).astype(
        jnp.bfloat16
    )[:, None]

    z_low, z_high = both_ways(scaled, shift_z)
    own_low, own_high = both_ways(scaled, shift_x)
    a = masked[None]
    a = jnp.concatenate([a, swap(a, 2)], 0)
    a = jnp.concatenate([a, swap(a, 4)], 0)
    own_far = far_halves(own_low, own_high, shift_x)
    a = jnp.concatenate([a, swap(a, 8)], 0)
    a_far = swap(a, 24)
    a_core = swap(a, 1)
    a_far_core = swap(a_far, 1)

    sums_shape = jax.ShapeDtypeStruct((outs, wide + BLK), jnp.float32)
    acts_all, a_inv = call(
        acts_kernel,
        (where, count),
        (a, a_far, a_core, a_far_core),
        (
            jax.ShapeDtypeStruct((32, TOK_DEV, wide), jnp.bfloat16),
            jax.ShapeDtypeStruct((wide // BLK, BLK, BLK), jnp.float32),
        ),
    )
    z_far = far_halves(z_low, z_high, shift_z)
    near = jnp.concatenate([z_low, z_high], 0)
    near_low, near_high = both_ways(near, shift_x)
    sums = call(
        functools.partial(first_kernel, 0),
        (where,),
        (acts_all, scaled, own_low, own_high, *own_far),
        sums_shape,
    )
    near_far = far_halves(near_low, near_high, shift_x)
    far = jnp.concatenate(z_far, 0)
    far_low, far_high = both_ways(far, shift_x)
    sums = call(
        functools.partial(more_kernel, 1),
        (where,),
        (acts_all, near, near_low, near_high, *near_far, sums),
        sums_shape,
    )
    far_far = far_halves(far_low, far_high, shift_x)
    return call(
        functools.partial(last_kernel, 2),
        (where, count),
        (acts_all, a_inv, far, far_low, far_high, *far_far, sums),
        jax.ShapeDtypeStruct((wide, outs), jnp.bfloat16),
        scratch=(pltpu.VMEM((outs, wide + BLK), jnp.float32),),
    )


def solution(mesh):
    placed = (P("dp", "inv"), P("inv", "dp"), P(), P())
    return jax.shard_map(
        local, mesh=mesh, in_specs=placed, out_specs=P("inv", "dp"), check_vma=False
    )
```

```python
import functools

import jax
import jax.numpy as jnp
from jax import lax
from jax.experimental import pallas as pl
from jax.experimental.pallas import tpu as pltpu
from jax.sharding import PartitionSpec as P

BLK = 128
TOK_DEV = 128
DAMPING = 0.001
VMEM_LIMIT = 40 * 1024 * 1024


def shift_x(step):
    return [(i, i // 4 * 4 + (i + step) % 4) for i in range(16)]


def shift_z(step):
    return [(i, (i // 4 + step) % 4 * 4 + i % 4) for i in range(16)]


def flip_dp(mask):
    return [(j, j ^ mask) for j in range(32)]


def hop(value, pairs):
    return lax.ppermute(value, "inv", pairs)


def swap(value, mask):
    return lax.ppermute(value, "dp", flip_dp(mask))


def both_ways(value, shift):
    return hop(value, shift(1)), hop(value, shift(-1))


def flip_x(mask):
    return [(i, i ^ mask) for i in range(16)]


def doubled(value, first):
    near = hop(value, flip_x(first))
    far = hop(jnp.concatenate([value, near], 0), flip_x(first ^ 2))
    return value, near, far


def far_halves(lower, upper, shift):
    half = lower.shape[0] // 2
    return hop(lower[:half], shift(1)), hop(upper[half:], shift(-1))


def eye(order):
    rows = lax.broadcasted_iota(jnp.int32, (order, order), 0)
    cols = lax.broadcasted_iota(jnp.int32, (order, order), 1)
    return rows == cols


def split(value, parts):
    out = []
    for n in range(parts):
        top = value.astype(jnp.bfloat16)
        out.append(top)
        if n < parts - 1:
            value = value - top.astype(jnp.float32)
    return out


def wide_dot(a, b):
    return jnp.dot(a, b, preferred_element_type=jnp.float32)


def dot_split(a, b):
    high, low = split(a, 2)
    b_high, b_low = split(b, 2)
    right = jnp.concatenate(
        [
            jnp.concatenate([b_high, b_low], 1),
            jnp.concatenate([b_high, jnp.zeros_like(b_low)], 1),
        ],
        0,
    )
    both = wide_dot(jnp.concatenate([high, low], 1), right)
    return both[:, :BLK] + both[:, BLK:]


def dot32(a, b):
    a1, a2, a3 = split(a, 3)
    b1, b2, b3 = split(b, 3)
    right = jnp.concatenate([b1, b2], 1)
    both = wide_dot(
        jnp.concatenate([a1, a2], 1), jnp.concatenate([right, right], 0)
    )
    rest = wide_dot(
        jnp.concatenate([a1, a3], 1), jnp.concatenate([b3, b1], 0)
    )
    return both[:, :BLK] + (both[:, BLK:] + rest)


def newton(covs):
    unit = eye(BLK)
    ident = unit.astype(jnp.float32)
    prods, approxes = [], []
    for cov in covs:
        trace = jnp.sum(jnp.where(unit, cov, 0.0))
        damped = cov + (DAMPING * (trace / BLK)) * ident
        total = jnp.sum(jnp.where(unit, damped, 0.0))
        prod = damped / total
        prods.append(prod)
        approxes.append((2.0 * ident - prod) / total)
    prods = [2.0 * d - dot_split(d, d) for d in prods]
    for step in range(6):
        both = [
            jnp.concatenate([x, d], 0) for x, d in zip(approxes, prods, strict=True)
        ]
        both = [
            2.0 * b - dot_split(b, d) for b, d in zip(both, prods, strict=True)
        ]
        approxes = [b[:BLK] for b in both]
        prods = [b[BLK:] for b in both]
    return [
        2.0 * x - dot_split(x, d) for x, d in zip(approxes, prods, strict=True)
    ]


def position():
    inv = lax.axis_index("inv")
    return lax.axis_index("dp"), inv // 4, inv % 4


def live_tokens(tokens_ref):
    return sum(tokens_ref[n] for n in range(tokens_ref.shape[0])).astype(jnp.float32)


def prepare_kernel(
    tokens_hbm,
    exps_hbm,
    acts_hbm,
    grads_hbm,
    masked_ref,
    scaled_ref,
    tokens_ref,
    exps_ref,
    acts_ref,
    grads_ref,
    sems,
):
    copies = [
        pltpu.make_async_copy(source, target, sems.at[n])
        for n, (source, target) in enumerate(
            (
                (tokens_hbm, tokens_ref),
                (exps_hbm, exps_ref),
                (grads_hbm, grads_ref),
                (acts_hbm, acts_ref),
            )
        )
    ]
    for copy in copies:
        copy.start()
    for copy in copies:
        copy.wait()
    inv = lax.axis_index("inv")
    row = lax.broadcasted_iota(jnp.int32, acts_ref.shape, 0)
    live = row < tokens_ref[lax.axis_index("dp")]
    masked_ref[...] = jnp.where(live, acts_ref[...].astype(jnp.float32), 0.0).astype(
        jnp.bfloat16
    )
    slot = lax.broadcasted_iota(jnp.int32, (TOK_DEV, BLK), 0)
    for n in range(grads_ref.shape[0] // TOK_DEV):
        shard = inv * 2 + n
        exps = exps_ref[pl.ds(shard, 1), :].astype(jnp.float32)
        scale = jnp.exp2(-jnp.broadcast_to(exps, (BLK, TOK_DEV)).T)
        scale = jnp.where(slot < tokens_ref[shard], scale, 0.0)
        scale = scale.astype(jnp.bfloat16).astype(jnp.float32)
        rows = slice(n * TOK_DEV, (n + 1) * TOK_DEV)
        for f in range(grads_ref.shape[1] // BLK):
            cols = slice(f * BLK, (f + 1) * BLK)
            scaled_ref[rows, cols] = (
                grads_ref[rows, cols].astype(jnp.float32) * scale
            ).astype(jnp.bfloat16)


def halves_kernel(low_ref, high_ref, first_ref, second_ref):
    half = first_ref.shape[0]
    first_ref[...] = low_ref[:half, :]
    second_ref[...] = high_ref[half:, :]


def join_kernel(low_ref, high_ref, both_ref, first_ref, second_ref):
    rows = low_ref.shape[0]
    both_ref[:rows, :] = low_ref[...]
    both_ref[rows:, :] = high_ref[...]
    halves_kernel(low_ref, high_ref, first_ref, second_ref)


def acts_kernel(tokens_ref, own_ref, core_ref, acts_ref, inv_ref):
    mine = lax.axis_index("dp")
    _, slots, wide = acts_ref.shape
    blocks = wide // BLK
    covs = [jnp.zeros((BLK, BLK), jnp.float32) for _ in range(blocks)]
    for ref, at, core in ((own_ref, 0, 0), (own_ref, 8, 0), (core_ref, 0, 1), (core_ref, 8, 1)):
        for k in range(at, at + 8):
            acts_ref[mine ^ (k * 2 + core)] = ref[k]
        rows = ref[at : at + 8].reshape(8 * slots, wide)
        flipped = rows.T
        for b in range(blocks):
            cols = slice(b * BLK, (b + 1) * BLK)
            covs[b] += jnp.dot(
                flipped[cols], rows[:, cols], preferred_element_type=jnp.float32
            )
    count = live_tokens(tokens_ref)
    for b, inverse in enumerate(newton([c / count for c in covs])):
        inv_ref[b] = inverse


def add_rows(acts_ref, piece, zh, x, half, sums, first=False):
    token = (zh & 3) * 8 + (x & 3) * 2
    if half is None:
        rows = acts_ref[pl.ds(token, 2)].reshape(2 * TOK_DEV, acts_ref.shape[2])
    else:
        rows = acts_ref[token + half]
    wide = rows.shape[1]
    flipped = piece.T
    main = jnp.dot(flipped, rows, preferred_element_type=jnp.float32)
    cov = [
        jnp.dot(
            flipped[f * BLK : (f + 1) * BLK],
            piece[:, f * BLK : (f + 1) * BLK],
            preferred_element_type=jnp.float32,
        )
        for f in range(piece.shape[1] // BLK)
    ]
    cov = jnp.concatenate(cov, 0)
    if first:
        sums[:, :wide] = main
        sums[:, wide:] = cov
    else:
        sums[:, :wide] += main
        sums[:, wide:] += cov


def own_kernel(acts_ref, own, near, far, sums):
    _, zh, x = position()
    rows = 2 * TOK_DEV
    add_rows(acts_ref, own[...], zh, x, None, sums, True)
    add_rows(acts_ref, near[...], zh, x ^ 1, None, sums)
    add_rows(acts_ref, far[:rows, :], zh, x ^ 3, None, sums)
    add_rows(acts_ref, far[rows:, :], zh, x ^ 2, None, sums)


def near_kernel(acts_ref, own, low, high, far_low, far_high, before, sums):
    _, zh, x = position()
    rows = 2 * TOK_DEV
    sums[...] = before[...]
    for ref, at in ((own, x), (low, x - 1), (high, x + 1)):
        add_rows(acts_ref, ref[:rows, :], zh - 1, at, None, sums)
        add_rows(acts_ref, ref[rows:, :], zh + 1, at, None, sums)
    add_rows(acts_ref, far_low[...], zh - 1, x + 2, None, sums)
    add_rows(acts_ref, far_high[...], zh + 1, x + 2, None, sums)


def last_kernel(
    tokens_ref, acts_ref, inv_ref, own, low, high, far_low, far_high, before, out_ref, sums
):
    _, zh, x = position()
    sums[...] = before[...]
    for ref, at in ((own, x), (low, x - 1), (high, x + 1)):
        add_rows(acts_ref, ref[...], zh + 2, at, None, sums)
    add_rows(acts_ref, far_low[...], zh + 2, x + 2, 0, sums)
    add_rows(acts_ref, far_high[...], zh + 2, x + 2, 1, sums)
    wide = acts_ref.shape[2]
    count = live_tokens(tokens_ref)
    outs = sums.shape[0]
    blocks = outs // BLK
    inverse = newton(
        [sums[f * BLK : (f + 1) * BLK, wide:] / count for f in range(blocks)]
    )
    lefts = []
    for b in range(wide // BLK):
        grad = sums[:, b * BLK : (b + 1) * BLK] / count
        lefts.append(dot32(grad, inv_ref[b].T))
    for f in range(blocks):
        rows = slice(f * BLK, (f + 1) * BLK)
        left = jnp.concatenate([part[rows].T for part in lefts], 0)
        out_ref[:, rows] = dot32(left, inverse[f]).astype(jnp.bfloat16)


def call(kernel, smem, vmem, shapes, micros, scratch=()):
    return pl.pallas_call(
        kernel,
        out_shape=shapes,
        in_specs=[pl.BlockSpec(memory_space=pltpu.SMEM)] * len(smem)
        + [pl.BlockSpec(memory_space=pltpu.VMEM)] * len(vmem),
        out_specs=jax.tree.map(
            lambda _: pl.BlockSpec(memory_space=pltpu.VMEM), shapes
        ),
        scratch_shapes=list(scratch),
        compiler_params=pltpu.CompilerParams(vmem_limit_bytes=VMEM_LIMIT),
        cost_estimate=pl.CostEstimate(
            flops=int(micros * 1.15e9), bytes_accessed=0, transcendentals=0
        ),
    )(*smem, *vmem)


def local(acts, grads_out, scale_exp, shard_tokens):
    rows, outs = grads_out.shape
    wide = acts.shape[1]
    sixteen = jnp.bfloat16
    exps = scale_exp.reshape(-1, TOK_DEV)
    operands = (shard_tokens, exps, acts, grads_out)
    masked, scaled = pl.pallas_call(
        prepare_kernel,
        out_shape=(
            jax.ShapeDtypeStruct(acts.shape, sixteen),
            jax.ShapeDtypeStruct(grads_out.shape, sixteen),
        ),
        in_specs=[pl.BlockSpec(memory_space=pltpu.HBM)] * 4,
        out_specs=(pl.BlockSpec(memory_space=pltpu.VMEM),) * 2,
        scratch_shapes=[pltpu.SMEM(shard_tokens.shape, jnp.int32)]
        + [pltpu.VMEM(v.shape, v.dtype) for v in (exps, acts, grads_out)]
        + [pltpu.SemaphoreType.DMA((4,))],
        compiler_params=pltpu.CompilerParams(vmem_limit_bytes=60 * 1024 * 1024),
    )(*operands)
    z_low, z_high = both_ways(scaled, shift_z)
    far_parts = far_halves(z_low, z_high, shift_z)
    own = doubled(scaled, 1)
    near = jnp.concatenate([z_low, z_high], 0)
    far = jnp.concatenate(far_parts, 0)
    far_low, far_high = both_ways(far, shift_x)
    a = masked[None]
    a = jnp.concatenate([a] + [swap(a, 2 * k) for k in (1, 2, 3)], 0)
    a = jnp.concatenate([a] + [swap(a, 8 * k) for k in (1, 2, 3)], 0)
    a, near = lax.optimization_barrier((a, near))
    a_core = swap(a, 1)
    near_low, near_high = both_ways(near, shift_x)
    near_far = far_halves(near_low, near_high, shift_x)
    acts_all, a_inv = call(
        acts_kernel,
        (shard_tokens,),
        (a, a_core),
        (
            jax.ShapeDtypeStruct((32, TOK_DEV, wide), sixteen),
            jax.ShapeDtypeStruct((wide // BLK, BLK, BLK), jnp.float32),
        ),
        4,
    )
    sums_shape = jax.ShapeDtypeStruct((outs, wide + BLK), jnp.float32)
    sums = call(own_kernel, (), (acts_all, *own), sums_shape, 2)
    far_low, far_high, near_far = lax.optimization_barrier(
        (far_low, far_high, near_far)
    )
    far_far = far_halves(far_low, far_high, shift_x)
    sums = call(
        near_kernel,
        (),
        (acts_all, near, near_low, near_high, *near_far, sums),
        sums_shape,
        2,
    )
    return call(
        last_kernel,
        (shard_tokens,),
        (acts_all, a_inv, far, far_low, far_high, *far_far, sums),
        jax.ShapeDtypeStruct((wide, outs), sixteen),
        10,
        scratch=(pltpu.VMEM((outs, wide + BLK), jnp.float32),),
    )


def solution(mesh):
    placed = (P("dp", "inv"), P("inv", "dp"), P(), P())
    return jax.shard_map(
        local, mesh=mesh, in_specs=placed, out_specs=P("inv", "dp"), check_vma=False
    )
```

```python
import functools

import jax
import jax.numpy as jnp
from jax import lax
from jax.experimental import pallas as pl
from jax.experimental.pallas import tpu as pltpu
from jax.sharding import PartitionSpec as P

BLK = 128
TOK_DEV = 128
DAMPING = 0.001
VMEM_LIMIT = 40 * 1024 * 1024


def shift_x(step):
    return [(i, i // 4 * 4 + (i + step) % 4) for i in range(16)]


def shift_z(step):
    return [(i, (i // 4 + step) % 4 * 4 + i % 4) for i in range(16)]


def flip_dp(mask):
    return [(j, j ^ mask) for j in range(32)]


def hop(value, pairs):
    return lax.ppermute(value, "inv", pairs)


def swap(value, mask):
    return lax.ppermute(value, "dp", flip_dp(mask))


def both_ways(value, shift):
    return hop(value, shift(1)), hop(value, shift(-1))


def flip_x(mask):
    return [(i, i ^ mask) for i in range(16)]


def doubled(value, first):
    near = hop(value, flip_x(first))
    far = hop(jnp.concatenate([value, near], 0), flip_x(first ^ 2))
    return value, near, far


def far_halves(lower, upper, shift):
    half = lower.shape[0] // 2
    return hop(lower[:half], shift(1)), hop(upper[half:], shift(-1))


def eye(order):
    rows = lax.broadcasted_iota(jnp.int32, (order, order), 0)
    cols = lax.broadcasted_iota(jnp.int32, (order, order), 1)
    return rows == cols


def split(value, parts):
    out = []
    for n in range(parts):
        top = value.astype(jnp.bfloat16)
        out.append(top)
        if n < parts - 1:
            value = value - top.astype(jnp.float32)
    return out


def wide_dot(a, b):
    return jnp.dot(a, b, preferred_element_type=jnp.float32)


def dot_split(a, b):
    high, low = split(a, 2)
    b_high, b_low = split(b, 2)
    right = jnp.concatenate(
        [
            jnp.concatenate([b_high, b_low], 1),
            jnp.concatenate([b_high, jnp.zeros_like(b_low)], 1),
        ],
        0,
    )
    both = wide_dot(jnp.concatenate([high, low], 1), right)
    return both[:, :BLK] + both[:, BLK:]


def dot32(a, b):
    a1, a2, a3 = split(a, 3)
    b1, b2, b3 = split(b, 3)
    right = jnp.concatenate([b1, b2], 1)
    both = wide_dot(
        jnp.concatenate([a1, a2], 1), jnp.concatenate([right, right], 0)
    )
    rest = wide_dot(
        jnp.concatenate([a1, a3], 1), jnp.concatenate([b3, b1], 0)
    )
    return both[:, :BLK] + (both[:, BLK:] + rest)


def newton(covs):
    unit = eye(BLK)
    ident = unit.astype(jnp.float32)
    prods, approxes = [], []
    for cov in covs:
        trace = jnp.sum(jnp.where(unit, cov, 0.0))
        damped = cov + (DAMPING * (trace / BLK)) * ident
        total = jnp.sum(jnp.where(unit, damped, 0.0))
        prod = damped / total
        prods.append(prod)
        approxes.append((2.0 * ident - prod) / total)
    prods = [2.0 * d - dot_split(d, d) for d in prods]
    for step in range(6):
        both = [
            jnp.concatenate([x, d], 0) for x, d in zip(approxes, prods, strict=True)
        ]
        both = [
            2.0 * b - dot_split(b, d) for b, d in zip(both, prods, strict=True)
        ]
        approxes = [b[:BLK] for b in both]
        prods = [b[BLK:] for b in both]
    return [
        2.0 * x - dot_split(x, d) for x, d in zip(approxes, prods, strict=True)
    ]


def position():
    inv = lax.axis_index("inv")
    return lax.axis_index("dp"), inv // 4, inv % 4


def live_tokens(tokens_ref):
    return sum(tokens_ref[n] for n in range(tokens_ref.shape[0])).astype(jnp.float32)


def prepare_kernel(
    tokens_hbm,
    exps_hbm,
    acts_hbm,
    grads_hbm,
    masked_ref,
    scaled_ref,
    tokens_ref,
    exps_ref,
    acts_ref,
    grads_ref,
    sems,
):
    copies = [
        pltpu.make_async_copy(source, target, sems.at[n])
        for n, (source, target) in enumerate(
            (
                (tokens_hbm, tokens_ref),
                (exps_hbm, exps_ref),
                (grads_hbm, grads_ref),
                (acts_hbm, acts_ref),
            )
        )
    ]
    for copy in copies:
        copy.start()
    for copy in copies:
        copy.wait()
    inv = lax.axis_index("inv")
    row = lax.broadcasted_iota(jnp.int32, acts_ref.shape, 0)
    live = row < tokens_ref[lax.axis_index("dp")]
    masked_ref[...] = jnp.where(live, acts_ref[...].astype(jnp.float32), 0.0).astype(
        jnp.bfloat16
    )
    slot = lax.broadcasted_iota(jnp.int32, (TOK_DEV, BLK), 0)
    for n in range(grads_ref.shape[0] // TOK_DEV):
        shard = inv * 2 + n
        exps = exps_ref[pl.ds(shard, 1), :].astype(jnp.float32)
        scale = jnp.exp2(-jnp.broadcast_to(exps, (BLK, TOK_DEV)).T)
        scale = jnp.where(slot < tokens_ref[shard], scale, 0.0)
        scale = scale.astype(jnp.bfloat16).astype(jnp.float32)
        rows = slice(n * TOK_DEV, (n + 1) * TOK_DEV)
        for f in range(grads_ref.shape[1] // BLK):
            cols = slice(f * BLK, (f + 1) * BLK)
            scaled_ref[rows, cols] = (
                grads_ref[rows, cols].astype(jnp.float32) * scale
            ).astype(jnp.bfloat16)


def halves_kernel(low_ref, high_ref, first_ref, second_ref):
    half = first_ref.shape[0]
    first_ref[...] = low_ref[:half, :]
    second_ref[...] = high_ref[half:, :]


def join_kernel(low_ref, high_ref, both_ref, first_ref, second_ref):
    rows = low_ref.shape[0]
    both_ref[:rows, :] = low_ref[...]
    both_ref[rows:, :] = high_ref[...]
    halves_kernel(low_ref, high_ref, first_ref, second_ref)


def acts_kernel(tokens_ref, own_ref, core_ref, acts_ref, inv_ref):
    mine = lax.axis_index("dp")
    _, slots, wide = acts_ref.shape
    blocks = wide // BLK
    covs = [jnp.zeros((BLK, BLK), jnp.float32) for _ in range(blocks)]
    for ref, at, core in ((own_ref, 0, 0), (own_ref, 8, 0), (core_ref, 0, 1), (core_ref, 8, 1)):
        for k in range(at, at + 8):
            acts_ref[mine ^ (k * 2 + core)] = ref[k]
        rows = ref[at : at + 8].reshape(8 * slots, wide)
        flipped = rows.T
        for b in range(blocks):
            cols = slice(b * BLK, (b + 1) * BLK)
            covs[b] += jnp.dot(
                flipped[cols], rows[:, cols], preferred_element_type=jnp.float32
            )
    count = live_tokens(tokens_ref)
    for b, inverse in enumerate(newton([c / count for c in covs])):
        inv_ref[b] = inverse


def add_rows(acts_ref, piece, zh, x, half, sums, first=False):
    token = (zh & 3) * 8 + (x & 3) * 2
    if half is None:
        rows = acts_ref[pl.ds(token, 2)].reshape(2 * TOK_DEV, acts_ref.shape[2])
    else:
        rows = acts_ref[token + half]
    wide = rows.shape[1]
    flipped = piece.T
    main = jnp.dot(flipped, rows, preferred_element_type=jnp.float32)
    cov = [
        jnp.dot(
            flipped[f * BLK : (f + 1) * BLK],
            piece[:, f * BLK : (f + 1) * BLK],
            preferred_element_type=jnp.float32,
        )
        for f in range(piece.shape[1] // BLK)
    ]
    cov = jnp.concatenate(cov, 0)
    if first:
        sums[:, :wide] = main
        sums[:, wide:] = cov
    else:
        sums[:, :wide] += main
        sums[:, wide:] += cov


def near_kernel(acts_ref, own, low, high, far_low, far_high, sums):
    _, zh, x = position()
    half = TOK_DEV
    for ref, at in ((own, x), (low, x - 1), (high, x + 1)):
        for n in range(3):
            piece = ref[2 * n * half : 2 * (n + 1) * half, :]
            add_rows(acts_ref, piece, zh + n - 1, at, None, sums, ref is own and not n)
    add_rows(acts_ref, far_low[: 2 * half, :], zh - 1, x + 2, None, sums)
    add_rows(acts_ref, far_low[2 * half :, :], zh, x + 2, 0, sums)
    add_rows(acts_ref, far_high[:half, :], zh, x + 2, 1, sums)
    add_rows(acts_ref, far_high[half:, :], zh + 1, x + 2, None, sums)


def last_kernel(
    tokens_ref, acts_ref, inv_ref, own, low, high, far_low, far_high, before, out_ref, sums
):
    _, zh, x = position()
    sums[...] = before[...]
    for ref, at in ((own, x), (low, x - 1), (high, x + 1)):
        add_rows(acts_ref, ref[...], zh + 2, at, None, sums)
    add_rows(acts_ref, far_low[...], zh + 2, x + 2, 0, sums)
    add_rows(acts_ref, far_high[...], zh + 2, x + 2, 1, sums)
    wide = acts_ref.shape[2]
    count = live_tokens(tokens_ref)
    outs = sums.shape[0]
    blocks = outs // BLK
    inverse = newton(
        [sums[f * BLK : (f + 1) * BLK, wide:] / count for f in range(blocks)]
    )
    lefts = []
    for b in range(wide // BLK):
        grad = sums[:, b * BLK : (b + 1) * BLK] / count
        lefts.append(dot32(grad, inv_ref[b].T))
    for f in range(blocks):
        rows = slice(f * BLK, (f + 1) * BLK)
        left = jnp.concatenate([part[rows].T for part in lefts], 0)
        out_ref[:, rows] = dot32(left, inverse[f]).astype(jnp.bfloat16)


def call(kernel, smem, vmem, shapes, micros, scratch=()):
    return pl.pallas_call(
        kernel,
        out_shape=shapes,
        in_specs=[pl.BlockSpec(memory_space=pltpu.SMEM)] * len(smem)
        + [pl.BlockSpec(memory_space=pltpu.VMEM)] * len(vmem),
        out_specs=jax.tree.map(
            lambda _: pl.BlockSpec(memory_space=pltpu.VMEM), shapes
        ),
        scratch_shapes=list(scratch),
        compiler_params=pltpu.CompilerParams(vmem_limit_bytes=VMEM_LIMIT),
        cost_estimate=pl.CostEstimate(
            flops=int(micros * 1.15e9), bytes_accessed=0, transcendentals=0
        ),
    )(*smem, *vmem)


def local(acts, grads_out, scale_exp, shard_tokens):
    rows, outs = grads_out.shape
    wide = acts.shape[1]
    sixteen = jnp.bfloat16
    exps = scale_exp.reshape(-1, TOK_DEV)
    operands = (shard_tokens, exps, acts, grads_out)
    masked, scaled = pl.pallas_call(
        prepare_kernel,
        out_shape=(
            jax.ShapeDtypeStruct(acts.shape, sixteen),
            jax.ShapeDtypeStruct(grads_out.shape, sixteen),
        ),
        in_specs=[pl.BlockSpec(memory_space=pltpu.HBM)] * 4,
        out_specs=(pl.BlockSpec(memory_space=pltpu.VMEM),) * 2,
        scratch_shapes=[pltpu.SMEM(shard_tokens.shape, jnp.int32)]
        + [pltpu.VMEM(v.shape, v.dtype) for v in (exps, acts, grads_out)]
        + [pltpu.SemaphoreType.DMA((4,))],
        compiler_params=pltpu.CompilerParams(vmem_limit_bytes=60 * 1024 * 1024),
    )(*operands)
    z_low, z_high = both_ways(scaled, shift_z)
    far_parts = far_halves(z_low, z_high, shift_z)
    near = jnp.concatenate([z_low, scaled, z_high], 0)
    far = jnp.concatenate(far_parts, 0)
    far_low, far_high = both_ways(far, shift_x)
    a = masked[None]
    a = jnp.concatenate([a] + [swap(a, 2 * k) for k in (1, 2, 3)], 0)
    a = jnp.concatenate([a] + [swap(a, 8 * k) for k in (1, 2, 3)], 0)
    a, near = lax.optimization_barrier((a, near))
    a_core = swap(a, 1)
    near_low, near_high = both_ways(near, shift_x)
    near_far = far_halves(near_low, near_high, shift_x)
    acts_all, a_inv = call(
        acts_kernel,
        (shard_tokens,),
        (a, a_core),
        (
            jax.ShapeDtypeStruct((32, TOK_DEV, wide), sixteen),
            jax.ShapeDtypeStruct((wide // BLK, BLK, BLK), jnp.float32),
        ),
        4,
    )
    sums_shape = jax.ShapeDtypeStruct((outs, wide + BLK), jnp.float32)
    far_low, far_high, near_far = lax.optimization_barrier(
        (far_low, far_high, near_far)
    )
    far_far = far_halves(far_low, far_high, shift_x)
    sums = call(
        near_kernel,
        (),
        (acts_all, near, near_low, near_high, *near_far),
        sums_shape,
        2,
    )
    return call(
        last_kernel,
        (shard_tokens,),
        (acts_all, a_inv, far, far_low, far_high, *far_far, sums),
        jax.ShapeDtypeStruct((wide, outs), sixteen),
        10,
        scratch=(pltpu.VMEM((outs, wide + BLK), jnp.float32),),
    )


def solution(mesh):
    placed = (P("dp", "inv"), P("inv", "dp"), P(), P())
    return jax.shard_map(
        local, mesh=mesh, in_specs=placed, out_specs=P("inv", "dp"), check_vma=False
    )
```

```python
import functools

import jax
import jax.numpy as jnp
from jax import lax
from jax.experimental import pallas as pl
from jax.experimental.pallas import tpu as pltpu
from jax.sharding import PartitionSpec as P

BLK = 128
TOK_DEV = 128
DAMPING = 0.001
VMEM_LIMIT = 40 * 1024 * 1024


def shift_x(step):
    return [(i, i // 4 * 4 + (i + step) % 4) for i in range(16)]


def shift_z(step):
    return [(i, (i // 4 + step) % 4 * 4 + i % 4) for i in range(16)]


def flip_dp(mask):
    return [(j, j ^ mask) for j in range(32)]


def hop(value, pairs):
    return lax.ppermute(value, "inv", pairs)


def swap(value, mask):
    return lax.ppermute(value, "dp", flip_dp(mask))


def both_ways(value, shift):
    return hop(value, shift(1)), hop(value, shift(-1))


def far_halves(lower, upper, shift):
    half = lower.shape[0] // 2
    return hop(lower[:half], shift(1)), hop(upper[half:], shift(-1))


def eye(order):
    rows = lax.broadcasted_iota(jnp.int32, (order, order), 0)
    cols = lax.broadcasted_iota(jnp.int32, (order, order), 1)
    return rows == cols


def split(value, parts):
    out = []
    for n in range(parts):
        top = value.astype(jnp.bfloat16)
        out.append(top)
        if n < parts - 1:
            value = value - top.astype(jnp.float32)
    return out


def wide_dot(a, b):
    return jnp.dot(a, b, preferred_element_type=jnp.float32)


def dot_split(a, b):
    high, low = split(a, 2)
    b_high, b_low = split(b, 2)
    right = jnp.concatenate(
        [
            jnp.concatenate([b_high, b_low], 1),
            jnp.concatenate([b_high, jnp.zeros_like(b_low)], 1),
        ],
        0,
    )
    both = wide_dot(jnp.concatenate([high, low], 1), right)
    return both[:, :BLK] + both[:, BLK:]


def dot32(a, b):
    a1, a2, a3 = split(a, 3)
    b1, b2, b3 = split(b, 3)
    right = jnp.concatenate([b1, b2], 1)
    both = wide_dot(
        jnp.concatenate([a1, a2], 1), jnp.concatenate([right, right], 0)
    )
    rest = wide_dot(
        jnp.concatenate([a1, a3], 1), jnp.concatenate([b3, b1], 0)
    )
    return both[:, :BLK] + (both[:, BLK:] + rest)


def newton(covs):
    unit = eye(BLK)
    ident = unit.astype(jnp.float32)
    prods, approxes = [], []
    for cov in covs:
        trace = jnp.sum(jnp.where(unit, cov, 0.0))
        damped = cov + (DAMPING * (trace / BLK)) * ident
        total = jnp.sum(jnp.where(unit, damped, 0.0))
        prod = damped / total
        prods.append(prod)
        approxes.append((2.0 * ident - prod) / total)
    prods = [2.0 * d - dot_split(d, d) for d in prods]
    for step in range(6):
        both = [
            jnp.concatenate([x, d], 0) for x, d in zip(approxes, prods, strict=True)
        ]
        both = [
            2.0 * b - dot_split(b, d) for b, d in zip(both, prods, strict=True)
        ]
        approxes = [b[:BLK] for b in both]
        prods = [b[BLK:] for b in both]
    return [
        2.0 * x - dot_split(x, d) for x, d in zip(approxes, prods, strict=True)
    ]


def position():
    inv = lax.axis_index("inv")
    return lax.axis_index("dp"), inv // 4, inv % 4


def live_tokens(tokens_ref):
    return sum(tokens_ref[n] for n in range(tokens_ref.shape[0])).astype(jnp.float32)


def weights_kernel(tokens_ref, exps_ref, weights_ref):
    slot = lax.broadcasted_iota(jnp.int32, (TOK_DEV, BLK), 0)
    for shard in range(weights_ref.shape[0]):
        exps = exps_ref[shard : shard + 1, :].astype(jnp.float32)
        scale = jnp.exp2(-jnp.broadcast_to(exps, (BLK, TOK_DEV)).T)
        scale = jnp.where(slot < tokens_ref[shard], scale, 0.0)
        weights_ref[shard] = scale.astype(jnp.bfloat16)


def halves_kernel(low_ref, high_ref, first_ref, second_ref):
    half = first_ref.shape[0]
    first_ref[...] = low_ref[:half, :]
    second_ref[...] = high_ref[half:, :]


def join_kernel(low_ref, high_ref, both_ref, first_ref, second_ref):
    rows = low_ref.shape[0]
    both_ref[:rows, :] = low_ref[...]
    both_ref[rows:, :] = high_ref[...]
    halves_kernel(low_ref, high_ref, first_ref, second_ref)


def acts_kernel(tokens_ref, own_ref, core_ref, acts_ref, inv_ref):
    mine = lax.axis_index("dp")
    _, slots, wide = acts_ref.shape
    blocks = wide // BLK
    covs = [jnp.zeros((BLK, BLK), jnp.float32) for _ in range(blocks)]
    slot = lax.broadcasted_iota(jnp.int32, (slots, wide), 0)
    for ref, at, core in ((own_ref, 0, 0), (own_ref, 8, 0), (core_ref, 0, 1), (core_ref, 8, 1)):
        live = []
        for k in range(at, at + 8):
            shard = mine ^ (k * 2 + core)
            part = jnp.where(slot < tokens_ref[shard], ref[k].astype(jnp.float32), 0.0)
            live.append(part.astype(jnp.bfloat16))
            acts_ref[shard] = live[-1]
        rows = jnp.concatenate(live, 0)
        flipped = rows.T
        for b in range(blocks):
            cols = slice(b * BLK, (b + 1) * BLK)
            covs[b] += jnp.dot(
                flipped[cols], rows[:, cols], preferred_element_type=jnp.float32
            )
    count = live_tokens(tokens_ref)
    for b, inverse in enumerate(newton([c / count for c in covs])):
        inv_ref[b] = inverse


def add_rows(acts_ref, weights_ref, piece, zh, x, half, sums, first=False):
    token = (zh & 3) * 8 + (x & 3) * 2
    if half is None:
        rows = acts_ref[pl.ds(token, 2)].reshape(2 * TOK_DEV, acts_ref.shape[2])
        weight = weights_ref[pl.ds(token, 2)].reshape(2 * TOK_DEV, BLK)
    else:
        rows = acts_ref[token + half]
        weight = weights_ref[token + half]
    piece = piece * jnp.concatenate([weight] * (piece.shape[1] // BLK), 1)
    wide = rows.shape[1]
    flipped = piece.T
    main = jnp.dot(flipped, rows, preferred_element_type=jnp.float32)
    cov = [
        jnp.dot(
            flipped[f * BLK : (f + 1) * BLK],
            piece[:, f * BLK : (f + 1) * BLK],
            preferred_element_type=jnp.float32,
        )
        for f in range(piece.shape[1] // BLK)
    ]
    cov = jnp.concatenate(cov, 0)
    if first:
        sums[:, :wide] = main
        sums[:, wide:] = cov
    else:
        sums[:, :wide] += main
        sums[:, wide:] += cov


def mixed_kernel(low_ref, high_ref, top_ref, bottom_ref, first_ref, second_ref):
    half, quarter = low_ref.shape[0] // 2, top_ref.shape[0]
    first_ref[:half, :] = low_ref[:half, :]
    second_ref[:half, :] = high_ref[half:, :]
    for ref in (first_ref, second_ref):
        ref[half : half + quarter, :] = top_ref[...]
        ref[half + quarter :, :] = bottom_ref[...]


def rest_kernel(low_ref, high_ref, first_ref, second_ref):
    half = first_ref.shape[0]
    first_ref[...] = low_ref[3 * half : 4 * half, :]
    second_ref[...] = high_ref[4 * half :, :]


def near_kernel(
    acts_ref, weights_ref, own, low, high, far_low, far_high, top, bottom, sums
):
    _, zh, x = position()
    half = TOK_DEV
    for ref, at in ((own, x), (low, x - 1), (high, x + 1)):
        for n in range(3):
            piece = ref[2 * n * half : 2 * (n + 1) * half, :]
            add_rows(acts_ref, weights_ref, piece, zh + n - 1, at, None, sums, ref is own and not n)
    add_rows(acts_ref, weights_ref, far_low[: 2 * half, :], zh - 1, x + 2, None, sums)
    add_rows(acts_ref, weights_ref, far_low[2 * half : 3 * half, :], zh, x + 2, 0, sums)
    add_rows(acts_ref, weights_ref, far_high[:half, :], zh, x + 2, 1, sums)
    add_rows(acts_ref, weights_ref, far_high[half : 3 * half, :], zh + 1, x + 2, None, sums)
    add_rows(acts_ref, weights_ref, top[...], zh + 2, x, 0, sums)
    add_rows(acts_ref, weights_ref, bottom[...], zh + 2, x, 1, sums)
    for ref, at in ((far_low, x - 1), (far_high, x + 1)):
        add_rows(acts_ref, weights_ref, ref[3 * half :, :], zh + 2, at, None, sums)


def last_kernel(
    tokens_ref,
    acts_ref,
    weights_ref,
    inv_ref,
    far_low,
    far_high,
    before,
    out_ref,
    sums,
):
    _, zh, x = position()
    sums[...] = before[...]
    add_rows(acts_ref, weights_ref, far_low[...], zh + 2, x + 2, 0, sums)
    add_rows(acts_ref, weights_ref, far_high[...], zh + 2, x + 2, 1, sums)
    wide = acts_ref.shape[2]
    count = live_tokens(tokens_ref)
    outs = sums.shape[0]
    blocks = outs // BLK
    inverse = newton(
        [sums[f * BLK : (f + 1) * BLK, wide:] / count for f in range(blocks)]
    )
    lefts = []
    for b in range(wide // BLK):
        grad = sums[:, b * BLK : (b + 1) * BLK] / count
        lefts.append(dot32(grad, inv_ref[b].T))
    for f in range(blocks):
        rows = slice(f * BLK, (f + 1) * BLK)
        left = jnp.concatenate([part[rows].T for part in lefts], 0)
        out_ref[:, rows] = dot32(left, inverse[f]).astype(jnp.bfloat16)


def call(kernel, smem, vmem, shapes, micros, scratch=()):
    return pl.pallas_call(
        kernel,
        out_shape=shapes,
        in_specs=[pl.BlockSpec(memory_space=pltpu.SMEM)] * len(smem)
        + [pl.BlockSpec(memory_space=pltpu.VMEM)] * len(vmem),
        out_specs=jax.tree.map(
            lambda _: pl.BlockSpec(memory_space=pltpu.VMEM), shapes
        ),
        scratch_shapes=list(scratch),
        compiler_params=pltpu.CompilerParams(vmem_limit_bytes=VMEM_LIMIT),
        cost_estimate=pl.CostEstimate(
            flops=int(micros * 1.15e9), bytes_accessed=0, transcendentals=0
        ),
    )(*smem, *vmem)


def local(acts, grads_out, scale_exp, shard_tokens):
    rows, outs = grads_out.shape
    wide = acts.shape[1]
    sixteen = jnp.bfloat16
    weights = call(
        weights_kernel,
        (shard_tokens,),
        (scale_exp.reshape(-1, TOK_DEV),),
        jax.ShapeDtypeStruct((shard_tokens.shape[0], TOK_DEV, BLK), sixteen),
        2,
    )
    z_low, z_high = both_ways(grads_out, shift_z)
    far_parts = far_halves(z_low, z_high, shift_z)
    near = jnp.concatenate([z_low, grads_out, z_high], 0)
    a = acts[None]
    a = jnp.concatenate([a] + [swap(a, 2 * k) for k in (1, 2, 3)], 0)
    a = jnp.concatenate([a] + [swap(a, 8 * k) for k in (1, 2, 3)], 0)
    a, _ = lax.optimization_barrier((a, near))
    a_core = swap(a, 1)
    near_low, near_high = both_ways(near, shift_x)
    mixed = jax.ShapeDtypeStruct((near.shape[0] // 2 + rows, outs), sixteen)
    first, second = call(
        mixed_kernel, (), (near_low, near_high, *far_parts), (mixed, mixed), 1
    )
    mixed_low, mixed_high = hop(first, shift_x(1)), hop(second, shift_x(-1))
    acts_all, a_inv = call(
        acts_kernel,
        (shard_tokens,),
        (a, a_core),
        (
            jax.ShapeDtypeStruct((32, TOK_DEV, wide), sixteen),
            jax.ShapeDtypeStruct((wide // BLK, BLK, BLK), jnp.float32),
        ),
        4,
    )
    sums_shape = jax.ShapeDtypeStruct((outs, wide + BLK), jnp.float32)
    far_half = jax.ShapeDtypeStruct((rows // 2, outs), sixteen)
    first, second = call(
        rest_kernel, (), (mixed_low, mixed_high), (far_half, far_half), 1
    )
    far_far = hop(first, shift_x(1)), hop(second, shift_x(-1))
    sums = call(
        near_kernel,
        (),
        (acts_all, weights, near, near_low, near_high, mixed_low, mixed_high, *far_parts),
        sums_shape,
        2,
    )
    return call(
        last_kernel,
        (shard_tokens,),
        (acts_all, weights, a_inv, *far_far, sums),
        jax.ShapeDtypeStruct((wide, outs), sixteen),
        10,
        scratch=(pltpu.VMEM((outs, wide + BLK), jnp.float32),),
    )


def solution(mesh):
    placed = (P("dp", "inv"), P("inv", "dp"), P(), P())
    return jax.shard_map(
        local, mesh=mesh, in_specs=placed, out_specs=P("inv", "dp"), check_vma=False
    )
```

```python
import jax
import jax.numpy as jnp
from jax import lax
from jax.experimental import pallas as pl
from jax.experimental.pallas import tpu as pltpu
from jax.sharding import PartitionSpec as P

BLK = 128
TOK_DEV = 128
DAMPING = 0.001
VMEM_LIMIT = 40 * 1024 * 1024


def shift_x(step):
    return [(i, i // 4 * 4 + (i + step) % 4) for i in range(16)]


def shift_z(step):
    return [(i, (i // 4 + step) % 4 * 4 + i % 4) for i in range(16)]


def flip_dp(mask):
    return [(j, j ^ mask) for j in range(32)]


def hop(value, pairs):
    return lax.ppermute(value, "inv", pairs)


def swap(value, mask):
    return lax.ppermute(value, "dp", flip_dp(mask))


def both_ways(value, shift):
    return hop(value, shift(1)), hop(value, shift(-1))


def far_halves(lower, upper, shift):
    half = lower.shape[0] // 2
    return hop(lower[:half], shift(1)), hop(upper[half:], shift(-1))


def eye(order):
    rows = lax.broadcasted_iota(jnp.int32, (order, order), 0)
    cols = lax.broadcasted_iota(jnp.int32, (order, order), 1)
    return rows == cols


def split(value, parts):
    out = []
    for n in range(parts):
        top = value.astype(jnp.bfloat16)
        out.append(top)
        if n < parts - 1:
            value = value - top.astype(jnp.float32)
    return out


def wide_dot(a, b):
    return jnp.dot(a, b, preferred_element_type=jnp.float32)


def dot_split(a, b):
    high, low = split(a, 2)
    b_high, b_low = split(b, 2)
    right = jnp.concatenate(
        [
            jnp.concatenate([b_high, b_low], 1),
            jnp.concatenate([b_high, jnp.zeros_like(b_low)], 1),
        ],
        0,
    )
    both = wide_dot(jnp.concatenate([high, low], 1), right)
    return both[:, :BLK] + both[:, BLK:]


def dot32(a, b):
    a1, a2, a3 = split(a, 3)
    b1, b2, b3 = split(b, 3)
    right = jnp.concatenate([b1, b2], 1)
    both = wide_dot(
        jnp.concatenate([a1, a2], 1), jnp.concatenate([right, right], 0)
    )
    rest = wide_dot(
        jnp.concatenate([a1, a3], 1), jnp.concatenate([b3, b1], 0)
    )
    return both[:, :BLK] + (both[:, BLK:] + rest)


def newton(covs):
    unit = eye(BLK)
    ident = unit.astype(jnp.float32)
    prods, approxes = [], []
    for cov in covs:
        trace = jnp.sum(jnp.where(unit, cov, 0.0))
        damped = cov + (DAMPING * (trace / BLK)) * ident
        total = jnp.sum(jnp.where(unit, damped, 0.0))
        prod = damped / total
        prods.append(prod)
        approxes.append((2.0 * ident - prod) / total)
    prods = [2.0 * d - dot_split(d, d) for d in prods]
    for step in range(6):
        both = [
            jnp.concatenate([x, d], 0) for x, d in zip(approxes, prods, strict=True)
        ]
        both = [
            2.0 * b - dot_split(b, d) for b, d in zip(both, prods, strict=True)
        ]
        approxes = [b[:BLK] for b in both]
        prods = [b[BLK:] for b in both]
    return [
        2.0 * x - dot_split(x, d) for x, d in zip(approxes, prods, strict=True)
    ]


def position():
    inv = lax.axis_index("inv")
    return lax.axis_index("dp"), inv // 4, inv % 4


def live_tokens(tokens_ref):
    return sum(tokens_ref[n] for n in range(tokens_ref.shape[0])).astype(jnp.float32)


def weights_kernel(tokens_ref, exps_ref, weights_ref):
    slot = lax.broadcasted_iota(jnp.int32, (TOK_DEV, BLK), 0)
    for shard in range(weights_ref.shape[0]):
        exps = exps_ref[shard : shard + 1, :].astype(jnp.float32)
        scale = jnp.exp2(-jnp.broadcast_to(exps, (BLK, TOK_DEV)).T)
        scale = jnp.where(slot < tokens_ref[shard], scale, 0.0)
        weights_ref[shard] = scale.astype(jnp.bfloat16)


def halves_kernel(low_ref, high_ref, first_ref, second_ref):
    half = first_ref.shape[0]
    first_ref[...] = low_ref[:half, :]
    second_ref[...] = high_ref[half:, :]


def join_kernel(low_ref, high_ref, both_ref, first_ref, second_ref):
    rows = low_ref.shape[0]
    both_ref[:rows, :] = low_ref[...]
    both_ref[rows:, :] = high_ref[...]
    halves_kernel(low_ref, high_ref, first_ref, second_ref)


def acts_kernel(
    tokens_ref, own_ref, core_ref, weights_ref, near, low, high, acts_ref, inv_ref, sums
):
    mine = lax.axis_index("dp")
    _, slots, wide = acts_ref.shape
    blocks = wide // BLK
    covs = [jnp.zeros((BLK, BLK), jnp.float32) for _ in range(blocks)]
    slot = lax.broadcasted_iota(jnp.int32, (slots, wide), 0)
    for ref, at, core in ((own_ref, 0, 0), (own_ref, 8, 0), (core_ref, 0, 1), (core_ref, 8, 1)):
        live = []
        for k in range(at, at + 8):
            shard = mine ^ (k * 2 + core)
            part = jnp.where(slot < tokens_ref[shard], ref[k].astype(jnp.float32), 0.0)
            live.append(part.astype(jnp.bfloat16))
            acts_ref[shard] = live[-1]
        rows = jnp.concatenate(live, 0)
        flipped = rows.T
        for b in range(blocks):
            cols = slice(b * BLK, (b + 1) * BLK)
            covs[b] += jnp.dot(
                flipped[cols], rows[:, cols], preferred_element_type=jnp.float32
            )
    count = live_tokens(tokens_ref)
    for b, inverse in enumerate(newton([c / count for c in covs])):
        inv_ref[b] = inverse
    add_near(acts_ref, weights_ref, near, low, high, sums)


def add_rows(acts_ref, weights_ref, piece, zh, x, half, sums, first=False, base=None):
    token = (zh & 3) * 8 + (x & 3) * 2
    if half is None:
        rows = acts_ref[pl.ds(token, 2)].reshape(2 * TOK_DEV, acts_ref.shape[2])
        weight = weights_ref[pl.ds(token, 2)].reshape(2 * TOK_DEV, BLK)
    else:
        rows = acts_ref[token + half]
        weight = weights_ref[token + half]
    piece = piece * jnp.concatenate([weight] * (piece.shape[1] // BLK), 1)
    wide = rows.shape[1]
    flipped = piece.T
    main = jnp.dot(flipped, rows, preferred_element_type=jnp.float32)
    cov = [
        jnp.dot(
            flipped[f * BLK : (f + 1) * BLK],
            piece[:, f * BLK : (f + 1) * BLK],
            preferred_element_type=jnp.float32,
        )
        for f in range(piece.shape[1] // BLK)
    ]
    cov = jnp.concatenate(cov, 0)
    if first:
        sums[:, :wide] = main
        sums[:, wide:] = cov
    else:
        base = sums if base is None else base
        sums[:, :wide] = base[:, :wide] + main
        sums[:, wide:] = base[:, wide:] + cov


def mixed_kernel(low_ref, high_ref, top_ref, bottom_ref, first_ref, second_ref):
    half, quarter = low_ref.shape[0] // 2, top_ref.shape[0]
    first_ref[:half, :] = low_ref[:half, :]
    second_ref[:half, :] = high_ref[half:, :]
    for ref in (first_ref, second_ref):
        ref[half : half + quarter, :] = top_ref[...]
        ref[half + quarter :, :] = bottom_ref[...]


def rest_kernel(low_ref, high_ref, first_ref, second_ref):
    half = first_ref.shape[0]
    first_ref[...] = low_ref[3 * half : 4 * half, :]
    second_ref[...] = high_ref[4 * half :, :]


def add_near(acts_ref, weights_ref, own, low, high, sums):
    _, zh, x = position()
    step = 2 * TOK_DEV
    for ref, at in ((own, x), (low, x - 1), (high, x + 1)):
        for n in range(3):
            piece = ref[n * step : (n + 1) * step, :]
            start = ref is own and not n
            add_rows(acts_ref, weights_ref, piece, zh + n - 1, at, None, sums, start)


def mixed_sums_kernel(
    acts_ref, weights_ref, far_low, far_high, top, bottom, before, sums
):
    _, zh, x = position()
    half = TOK_DEV
    base = before
    for piece, z, at in (
        (far_low[: 2 * half, :], zh - 1, x + 2),
        (jnp.concatenate([far_low[2 * half : 3 * half, :], far_high[:half, :]], 0), zh, x + 2),
        (far_high[half : 3 * half, :], zh + 1, x + 2),
        (jnp.concatenate([top[...], bottom[...]], 0), zh + 2, x),
        (far_low[3 * half :, :], zh + 2, x - 1),
        (far_high[3 * half :, :], zh + 2, x + 1),
    ):
        add_rows(acts_ref, weights_ref, piece, z, at, None, sums, base=base)
        base = None


def last_kernel(
    tokens_ref,
    acts_ref,
    weights_ref,
    inv_ref,
    far_low,
    far_high,
    before,
    out_ref,
    sums,
):
    _, zh, x = position()
    piece = jnp.concatenate([far_low[...], far_high[...]], 0)
    add_rows(
        acts_ref, weights_ref, piece, zh + 2, x + 2, None, sums, base=before
    )
    wide = acts_ref.shape[2]
    count = live_tokens(tokens_ref)
    outs = sums.shape[0]
    blocks = outs // BLK
    inverse = newton(
        [sums[f * BLK : (f + 1) * BLK, wide:] / count for f in range(blocks)]
    )
    lefts = []
    for b in range(wide // BLK):
        grad = sums[:, b * BLK : (b + 1) * BLK] / count
        lefts.append(dot32(grad, inv_ref[b].T))
    for f in range(blocks):
        rows = slice(f * BLK, (f + 1) * BLK)
        left = jnp.concatenate([part[rows].T for part in lefts], 0)
        out_ref[:, rows] = dot32(left, inverse[f]).astype(jnp.bfloat16)


def call(kernel, smem, vmem, shapes, micros, scratch=()):
    return pl.pallas_call(
        kernel,
        out_shape=shapes,
        in_specs=[pl.BlockSpec(memory_space=pltpu.SMEM)] * len(smem)
        + [pl.BlockSpec(memory_space=pltpu.VMEM)] * len(vmem),
        out_specs=jax.tree.map(
            lambda _: pl.BlockSpec(memory_space=pltpu.VMEM), shapes
        ),
        scratch_shapes=list(scratch),
        compiler_params=pltpu.CompilerParams(vmem_limit_bytes=VMEM_LIMIT),
        cost_estimate=pl.CostEstimate(
            flops=int(micros * 1.15e9), bytes_accessed=0, transcendentals=0
        ),
    )(*smem, *vmem)


def local(acts, grads_out, scale_exp, shard_tokens):
    rows, outs = grads_out.shape
    wide = acts.shape[1]
    sixteen = jnp.bfloat16
    weights = call(
        weights_kernel,
        (shard_tokens,),
        (scale_exp.reshape(-1, TOK_DEV),),
        jax.ShapeDtypeStruct((shard_tokens.shape[0], TOK_DEV, BLK), sixteen),
        2,
    )
    z_low, z_high = both_ways(grads_out, shift_z)
    far_parts = far_halves(z_low, z_high, shift_z)
    near = jnp.concatenate([z_low, grads_out, z_high], 0)
    a = acts[None]
    a = jnp.concatenate([a] + [swap(a, 2 * k) for k in (1, 2, 3)], 0)
    a = jnp.concatenate([a] + [swap(a, 8 * k) for k in (1, 2, 3)], 0)
    a, _ = lax.optimization_barrier((a, near))
    a_core = swap(a, 1)
    near_low, near_high = both_ways(near, shift_x)
    mixed = jax.ShapeDtypeStruct((near.shape[0] // 2 + rows, outs), sixteen)
    first, second = call(
        mixed_kernel, (), (near_low, near_high, *far_parts), (mixed, mixed), 1
    )
    mixed_low, mixed_high = hop(first, shift_x(1)), hop(second, shift_x(-1))
    sums_shape = jax.ShapeDtypeStruct((outs, wide + BLK), jnp.float32)
    acts_all, a_inv, sums = call(
        acts_kernel,
        (shard_tokens,),
        (a, a_core, weights, near, near_low, near_high),
        (
            jax.ShapeDtypeStruct((32, TOK_DEV, wide), sixteen),
            jax.ShapeDtypeStruct((wide // BLK, BLK, BLK), jnp.float32),
            sums_shape,
        ),
        4,
    )
    far_half = jax.ShapeDtypeStruct((rows // 2, outs), sixteen)
    first, second = call(
        rest_kernel, (), (mixed_low, mixed_high), (far_half, far_half), 1
    )
    far_far = hop(first, shift_x(1)), hop(second, shift_x(-1))
    sums = call(
        mixed_sums_kernel,
        (),
        (acts_all, weights, mixed_low, mixed_high, *far_parts, sums),
        sums_shape,
        2,
    )
    return call(
        last_kernel,
        (shard_tokens,),
        (acts_all, weights, a_inv, *far_far, sums),
        jax.ShapeDtypeStruct((wide, outs), sixteen),
        10,
        scratch=(pltpu.VMEM((outs, wide + BLK), jnp.float32),),
    )


def solution(mesh):
    placed = (P("dp", "inv"), P("inv", "dp"), P(), P())
    return jax.shard_map(
        local, mesh=mesh, in_specs=placed, out_specs=P("inv", "dp"), check_vma=False
    )
```

```python
import jax
import jax.numpy as jnp
from jax import lax
from jax.experimental import pallas as pl
from jax.experimental.pallas import tpu as pltpu
from jax.sharding import PartitionSpec as P

BLK = 128
TOK_DEV = 128
DAMPING = 0.001
VMEM_LIMIT = 28 * 1024 * 1024


def shift_x(step):
    return [(i, i // 4 * 4 + (i + step) % 4) for i in range(16)]


def shift_z(step):
    return [(i, (i // 4 + step) % 4 * 4 + i % 4) for i in range(16)]


def flip_dp(mask):
    return [(j, j ^ mask) for j in range(32)]


def hop(value, pairs):
    return lax.ppermute(value, "inv", pairs)


def swap(value, mask):
    return lax.ppermute(value, "dp", flip_dp(mask))


def both_ways(value, shift):
    return hop(value, shift(1)), hop(value, shift(-1))


def far_halves(lower, upper, shift):
    half = lower.shape[0] // 2
    return hop(lower[:half], shift(1)), hop(upper[half:], shift(-1))


def eye(order):
    rows = lax.broadcasted_iota(jnp.int32, (order, order), 0)
    cols = lax.broadcasted_iota(jnp.int32, (order, order), 1)
    return rows == cols


def split(value, parts):
    out = []
    for n in range(parts):
        top = value.astype(jnp.bfloat16)
        out.append(top)
        if n < parts - 1:
            value = value - top.astype(jnp.float32)
    return out


def wide_dot(a, b):
    return jnp.dot(a, b, preferred_element_type=jnp.float32)


def dot_split(a, b):
    high, low = split(a, 2)
    b_high, b_low = split(b, 2)
    right = jnp.concatenate(
        [
            jnp.concatenate([b_high, b_low], 1),
            jnp.concatenate([b_high, jnp.zeros_like(b_low)], 1),
        ],
        0,
    )
    both = wide_dot(jnp.concatenate([high, low], 1), right)
    return both[:, :BLK] + both[:, BLK:]


def dot32(a, b):
    a1, a2, a3 = split(a, 3)
    b1, b2, b3 = split(b, 3)
    right = jnp.concatenate([b1, b2], 1)
    both = wide_dot(
        jnp.concatenate([a1, a2], 1), jnp.concatenate([right, right], 0)
    )
    rest = wide_dot(
        jnp.concatenate([a1, a3], 1), jnp.concatenate([b3, b1], 0)
    )
    return both[:, :BLK] + (both[:, BLK:] + rest)


def newton(covs):
    unit = eye(BLK)
    ident = unit.astype(jnp.float32)
    prods, approxes = [], []
    for cov in covs:
        trace = jnp.sum(jnp.where(unit, cov, 0.0))
        damped = cov + (DAMPING * (trace / BLK)) * ident
        total = jnp.sum(jnp.where(unit, damped, 0.0))
        prod = damped / total
        prods.append(prod)
        approxes.append((2.0 * ident - prod) / total)
    prods = [2.0 * d - dot_split(d, d) for d in prods]
    for step in range(6):
        both = [
            jnp.concatenate([x, d], 0) for x, d in zip(approxes, prods, strict=True)
        ]
        both = [
            2.0 * b - dot_split(b, d) for b, d in zip(both, prods, strict=True)
        ]
        approxes = [b[:BLK] for b in both]
        prods = [b[BLK:] for b in both]
    return [
        2.0 * x - dot_split(x, d) for x, d in zip(approxes, prods, strict=True)
    ]


def position():
    inv = lax.axis_index("inv")
    return lax.axis_index("dp"), inv // 4, inv % 4


def live_tokens(tokens_ref):
    return sum(tokens_ref[n] for n in range(tokens_ref.shape[0])).astype(jnp.float32)


def weights_kernel(tokens_ref, exps_ref, weights_ref):
    slot = lax.broadcasted_iota(jnp.int32, (TOK_DEV, BLK), 0)
    for shard in range(weights_ref.shape[0]):
        exps = exps_ref[shard : shard + 1, :].astype(jnp.float32)
        scale = jnp.exp2(-jnp.broadcast_to(exps, (BLK, TOK_DEV)).T)
        scale = jnp.where(slot < tokens_ref[shard], scale, 0.0)
        weights_ref[shard] = scale.astype(jnp.bfloat16)


def halves_kernel(low_ref, high_ref, first_ref, second_ref):
    half = first_ref.shape[0]
    first_ref[...] = low_ref[:half, :]
    second_ref[...] = high_ref[half:, :]


def join_kernel(low_ref, high_ref, both_ref, first_ref, second_ref):
    rows = low_ref.shape[0]
    both_ref[:rows, :] = low_ref[...]
    both_ref[rows:, :] = high_ref[...]
    halves_kernel(low_ref, high_ref, first_ref, second_ref)


def acts_kernel(
    tokens_ref, own_ref, core_ref, weights_ref, near, low, high, acts_ref, inv_ref, sums
):
    mine = lax.axis_index("dp")
    _, slots, wide = acts_ref.shape
    blocks = wide // BLK
    covs = [jnp.zeros((BLK, BLK), jnp.float32) for _ in range(blocks)]
    slot = lax.broadcasted_iota(jnp.int32, (slots, wide), 0)
    for ref, at, core in ((own_ref, 0, 0), (own_ref, 8, 0), (core_ref, 0, 1), (core_ref, 8, 1)):
        live = []
        for k in range(at, at + 8):
            shard = mine ^ (k * 2 + core)
            part = jnp.where(slot < tokens_ref[shard], ref[k].astype(jnp.float32), 0.0)
            live.append(part.astype(jnp.bfloat16))
            acts_ref[shard] = live[-1]
        rows = jnp.concatenate(live, 0)
        flipped = rows.T
        for b in range(blocks):
            cols = slice(b * BLK, (b + 1) * BLK)
            covs[b] += jnp.dot(
                flipped[cols], rows[:, cols], preferred_element_type=jnp.float32
            )
    count = live_tokens(tokens_ref)
    for b, inverse in enumerate(newton([c / count for c in covs])):
        inv_ref[b] = inverse
    add_near(acts_ref, weights_ref, near, low, high, sums)


def add_rows(acts_ref, weights_ref, piece, zh, x, half, sums, first=False, base=None):
    token = (zh & 3) * 8 + (x & 3) * 2
    if half is None:
        rows = acts_ref[pl.ds(token, 2)].reshape(2 * TOK_DEV, acts_ref.shape[2])
        weight = weights_ref[pl.ds(token, 2)].reshape(2 * TOK_DEV, BLK)
    else:
        rows = acts_ref[token + half]
        weight = weights_ref[token + half]
    piece = piece * jnp.concatenate([weight] * (piece.shape[1] // BLK), 1)
    wide = rows.shape[1]
    flipped = piece.T
    main = jnp.dot(flipped, rows, preferred_element_type=jnp.float32)
    cov = [
        jnp.dot(
            flipped[f * BLK : (f + 1) * BLK],
            piece[:, f * BLK : (f + 1) * BLK],
            preferred_element_type=jnp.float32,
        )
        for f in range(piece.shape[1] // BLK)
    ]
    cov = jnp.concatenate(cov, 0)
    if first:
        sums[:, :wide] = main
        sums[:, wide:] = cov
    else:
        base = sums if base is None else base
        sums[:, :wide] = base[:, :wide] + main
        sums[:, wide:] = base[:, wide:] + cov


def mixed_kernel(low_ref, high_ref, top_ref, bottom_ref, first_ref, second_ref):
    half, quarter = low_ref.shape[0] // 2, top_ref.shape[0]
    first_ref[:half, :] = low_ref[:half, :]
    second_ref[:half, :] = high_ref[half:, :]
    for ref in (first_ref, second_ref):
        ref[half : half + quarter, :] = top_ref[...]
        ref[half + quarter :, :] = bottom_ref[...]


def rest_kernel(low_ref, high_ref, first_ref, second_ref):
    half = first_ref.shape[0]
    first_ref[...] = low_ref[3 * half : 4 * half, :]
    second_ref[...] = high_ref[4 * half :, :]


def add_near(acts_ref, weights_ref, own, low, high, sums):
    _, zh, x = position()
    step = 2 * TOK_DEV
    for ref, at in ((own, x), (low, x - 1), (high, x + 1)):
        for n in range(3):
            piece = ref[n * step : (n + 1) * step, :]
            start = ref is own and not n
            add_rows(acts_ref, weights_ref, piece, zh + n - 1, at, None, sums, start)


def mixed_sums_kernel(
    acts_ref, weights_ref, far_low, far_high, top, bottom, before, sums
):
    _, zh, x = position()
    half = TOK_DEV
    base = before
    for piece, z, at in (
        (far_low[: 2 * half, :], zh - 1, x + 2),
        (jnp.concatenate([far_low[2 * half : 3 * half, :], far_high[:half, :]], 0), zh, x + 2),
        (far_high[half : 3 * half, :], zh + 1, x + 2),
        (jnp.concatenate([top[...], bottom[...]], 0), zh + 2, x),
        (far_low[3 * half :, :], zh + 2, x - 1),
        (far_high[3 * half :, :], zh + 2, x + 1),
    ):
        add_rows(acts_ref, weights_ref, piece, z, at, None, sums, base=base)
        base = None


def last_kernel(
    tokens_ref,
    acts_ref,
    weights_ref,
    inv_ref,
    far_low,
    far_high,
    before,
    out_ref,
    sums,
):
    _, zh, x = position()
    piece = jnp.concatenate([far_low[...], far_high[...]], 0)
    add_rows(
        acts_ref, weights_ref, piece, zh + 2, x + 2, None, sums, base=before
    )
    wide = acts_ref.shape[2]
    count = live_tokens(tokens_ref)
    outs = sums.shape[0]
    blocks = outs // BLK
    inverse = newton(
        [sums[f * BLK : (f + 1) * BLK, wide:] / count for f in range(blocks)]
    )
    lefts = []
    for b in range(wide // BLK):
        grad = sums[:, b * BLK : (b + 1) * BLK] / count
        lefts.append(dot32(grad, inv_ref[b].T))
    for f in range(blocks):
        rows = slice(f * BLK, (f + 1) * BLK)
        left = jnp.concatenate([part[rows].T for part in lefts], 0)
        out_ref[:, rows] = dot32(left, inverse[f]).astype(jnp.bfloat16)


def call(kernel, smem, vmem, shapes, micros, scratch=()):
    return pl.pallas_call(
        kernel,
        out_shape=shapes,
        in_specs=[pl.BlockSpec(memory_space=pltpu.SMEM)] * len(smem)
        + [pl.BlockSpec(memory_space=pltpu.VMEM)] * len(vmem),
        out_specs=jax.tree.map(
            lambda _: pl.BlockSpec(memory_space=pltpu.VMEM), shapes
        ),
        scratch_shapes=list(scratch),
        compiler_params=pltpu.CompilerParams(vmem_limit_bytes=VMEM_LIMIT),
        cost_estimate=pl.CostEstimate(
            flops=int(micros * 1.15e9), bytes_accessed=0, transcendentals=0
        ),
    )(*smem, *vmem)


def local(acts, grads_out, scale_exp, shard_tokens):
    rows, outs = grads_out.shape
    wide = acts.shape[1]
    sixteen = jnp.bfloat16
    weights = call(
        weights_kernel,
        (shard_tokens,),
        (scale_exp.reshape(-1, TOK_DEV),),
        jax.ShapeDtypeStruct((shard_tokens.shape[0], TOK_DEV, BLK), sixteen),
        2,
    )
    z_low, z_high = both_ways(grads_out, shift_z)
    far_parts = far_halves(z_low, z_high, shift_z)
    near = jnp.concatenate([z_low, grads_out, z_high], 0)
    a = acts[None]
    a = jnp.concatenate([a] + [swap(a, 2 * k) for k in (1, 2, 3)], 0)
    a = jnp.concatenate([a] + [swap(a, 8 * k) for k in (1, 2, 3)], 0)
    a, _ = lax.optimization_barrier((a, near))
    a_core = swap(a, 1)
    near_low, near_high = both_ways(near, shift_x)
    mixed = jax.ShapeDtypeStruct((near.shape[0] // 2 + rows, outs), sixteen)
    first, second = call(
        mixed_kernel, (), (near_low, near_high, *far_parts), (mixed, mixed), 1
    )
    mixed_low, mixed_high = hop(first, shift_x(1)), hop(second, shift_x(-1))
    sums_shape = jax.ShapeDtypeStruct((outs, wide + BLK), jnp.float32)
    acts_all, a_inv, sums = call(
        acts_kernel,
        (shard_tokens,),
        (a, a_core, weights, near, near_low, near_high),
        (
            jax.ShapeDtypeStruct((32, TOK_DEV, wide), sixteen),
            jax.ShapeDtypeStruct((wide // BLK, BLK, BLK), jnp.float32),
            sums_shape,
        ),
        4,
    )
    far_half = jax.ShapeDtypeStruct((rows // 2, outs), sixteen)
    first, second = call(
        rest_kernel, (), (mixed_low, mixed_high), (far_half, far_half), 1
    )
    far_far = hop(first, shift_x(1)), hop(second, shift_x(-1))
    sums = call(
        mixed_sums_kernel,
        (),
        (acts_all, weights, mixed_low, mixed_high, *far_parts, sums),
        sums_shape,
        2,
    )
    return call(
        last_kernel,
        (shard_tokens,),
        (acts_all, weights, a_inv, *far_far, sums),
        jax.ShapeDtypeStruct((wide, outs), sixteen),
        10,
        scratch=(pltpu.VMEM((outs, wide + BLK), jnp.float32),),
    )


def solution(mesh):
    placed = (P("dp", "inv"), P("inv", "dp"), P(), P())
    return jax.shard_map(
        local, mesh=mesh, in_specs=placed, out_specs=P("inv", "dp"), check_vma=False
    )
```
